32 devices in a mesh: cases: 2 (over y), nodes: 4 (over z), fsdp: 2 (over x), rep: 2 (over core).
Axes of the slice: x: 2, y: 2, z: 4, core: 2. Of those that a mesh axis runs over, the one named last changes fastest.
Arguments:
- features: bfloat16 [8, 1024, 512], P(('cases', 'fsdp', 'rep'), 'nodes'), parts along dimension 0
- cotangent: bfloat16 [8, 1024, 512], P(('cases', 'fsdp', 'rep'), 'nodes'), parts along dimension 0
- weights: bfloat16 [2, 2, 512, 512], P(None, None, 'fsdp'), may hold values from -0.25 to 0.25
- gains: float32 [2, 512], replicated, may hold values from 0.25 to 1.75
- tile_pairs: int32 [4, 2, 12], P('nodes'), may hold values from 0 to 3, as said below
- halo_send: int32 [4, 2, 1], P('nodes'), may hold values from 0 to 1, as said below
- entry_counts: int32 [4], P('nodes'), may hold values from 2 to 12, as said below
- tile_values: bfloat16 [4, 12, 128, 128], P('nodes'), may hold values from -0.375 to 0.375
Outputs:
- output: bfloat16 [8, 1024, 512], P(('cases', 'fsdp', 'rep'), 'nodes'), parts along dimension 0
- weight_grads: float32 [512, 4, 2, 512], P('fsdp', 'cases'), parts along dimension 1
- gain_grads: float32 [4, 512], P('cases'), parts along dimension 0
The draws below stay inside these ranges and needn't reach their ends.
There are 2 independent parts, one for each index of `cases`. The reference program is written for one: setup_inputs(seed, part) draws one part's arguments, and reference() takes and returns one part's arrays. A program takes and returns all parts, laid end to end along the dimension named above; an argument that names none is the same for every part. Nothing has to cross between parts.
Inputs may be any that keep to these rules, and one draw needn't show every extreme that they name: `tile_pairs`: entries 0 to 1 of every partition name the column tiles 2 to 3 in order; row tiles are below 2. Each list halo_send[q, k] holds 1 distinct tiles. `entry_counts`: exactly one partition has all 12 entries live; every other one at most 6.
All inputs are finite; a program needn't handle non-finite values.
Results may differ from the reference program's by a relative error of at most 0.014.
Values may be sent and summed in bfloat16 or wider, within the bound.
A program may use at most 64 MiB of HBM per device.

```python
import math
import jax
import jax.numpy as jnp
from jax import lax

D = 512
TILE = 128
TILES_DEV = 2
HALO_TILES = 1
ENTRIES_DEV = 12
LAYERS = 2
PARTITIONS = 4
NTILES = 8
NODES = 1024
SAMPLES = 4
N_NODES = 4


def draw_features(key, part):
    keys = jax.random.split(key, 3)
    spread_log = math.log(10.0)
    row_scale = jnp.exp(jax.random.uniform(keys[0], (SAMPLES, NODES, 1), jnp.float32) * spread_log) / math.sqrt(10.0)
    col_scale = jnp.exp(jax.random.uniform(keys[1], (1, 1, D), jnp.float32) * spread_log) / math.sqrt(10.0)
    values = jax.random.truncated_normal(keys[2], -4.0, 4.0, (SAMPLES, NODES, D), jnp.float32) * row_scale * col_scale
    return values.astype(jnp.bfloat16)


def draw_cotangent(key, part):
    keys = jax.random.split(key, 1)
    node_pos = jnp.arange(NODES, dtype=jnp.float32)[None, :, None] / NODES
    rising = (1.0 + 2.0 * node_pos) / math.sqrt(SAMPLES * NODES)
    values = jax.random.truncated_normal(keys[0], -4.0, 4.0, (SAMPLES, NODES, D), jnp.float32) * rising
    return values.astype(jnp.bfloat16)


def draw_tile_pairs(key, part):
    keys = jax.random.split(key, 2)
    row_ids = jax.random.randint(keys[0], (N_NODES, ENTRIES_DEV), 0, TILES_DEV)
    col_ids = jax.random.randint(keys[1], (N_NODES, ENTRIES_DEV), 0, TILES_DEV + 2 * HALO_TILES)
    fixed_cols = TILES_DEV + jnp.arange(2 * HALO_TILES)
    col_ids = col_ids.at[:, :2 * HALO_TILES].set(jnp.broadcast_to(fixed_cols[None, :], (N_NODES, 2 * HALO_TILES)))
    return jnp.stack([row_ids, col_ids], axis=1).astype(jnp.int32)


def draw_halo_send(key, part):
    keys = jax.random.split(key, N_NODES * 2)
    picked = jax.vmap(lambda single: jax.random.permutation(single, TILES_DEV)[:HALO_TILES])(keys)
    return picked.reshape(N_NODES, 2, HALO_TILES).astype(jnp.int32)


def draw_entry_counts(key, part):
    keys = jax.random.split(key, 2)
    counts = jax.random.randint(keys[0], (N_NODES,), 2 * HALO_TILES, ENTRIES_DEV // 2 + 1)
    busiest = jax.random.randint(keys[1], (), 0, N_NODES)
    return jnp.where(jnp.arange(N_NODES) == busiest, ENTRIES_DEV, counts).astype(jnp.int32)


def block_levels(stream_key, shape, cuts, least, top_value):
    level = 1.0
    for dim, shards_of in cuts:
        heights = jax.random.uniform(jax.random.fold_in(jax.random.fold_in(stream_key, 6), dim), (shards_of,), jnp.float32, least / len(cuts), top_value / len(cuts))
        level = level * jnp.repeat(jnp.exp(heights), shape[dim] // shards_of).reshape((-1,) + (1,) * (len(shape) - 1 - dim))
    return level


def centred(key, dims, width, bound, pieces=(), kind=jnp.bfloat16):
    factor_of = block_levels(key, dims, pieces, -0.22, 0.18) if pieces else 1.0
    values = jax.random.normal(key, dims, jnp.float32) * width * factor_of
    return jnp.minimum(jnp.maximum(values, -bound), bound).astype(kind)


def setup_inputs(seed: int = 0, part: int = 0) -> dict:
    key_list = jax.random.split(jax.random.key(seed), 9)
    part_keys = jax.random.split(jax.random.fold_in(key_list[8], part), 9)
    features = draw_features(jax.random.fold_in(jax.random.fold_in(key_list[8], part), 71), part)
    cotangent = draw_cotangent(jax.random.fold_in(jax.random.fold_in(key_list[8], part), 71), part)
    weights = centred(key_list[2], (LAYERS, 2, D, D), D ** -0.5, 0.25, ((2, 2),))
    gains = jnp.clip(1.0 + 0.15 * jax.random.normal(key_list[3], (LAYERS, D), jnp.float32), 0.25, 1.75)
    tile_pairs = draw_tile_pairs(jax.random.fold_in(key_list[8], 71), part)
    halo_send = draw_halo_send(jax.random.fold_in(key_list[8], 71), part)
    entry_counts = draw_entry_counts(jax.random.fold_in(key_list[8], 71), part)
    tile_values = centred(key_list[7], (PARTITIONS, ENTRIES_DEV, TILE, TILE), (2 * TILE) ** -0.5, 0.375, ((0, 4),))
    return dict(features=features, cotangent=cotangent, weights=weights, gains=gains, tile_pairs=tile_pairs, halo_send=halo_send, entry_counts=entry_counts, tile_values=tile_values)


EPSILON = 1e-05

def silu_slope(values):
    sigmoid_part = jax.nn.sigmoid(values)
    return sigmoid_part * (1.0 + values * (1.0 - sigmoid_part))

def column_table(halo_send):
    part_ids = jnp.arange(PARTITIONS, dtype=jnp.int32)
    local_ids = part_ids[:, None] * TILES_DEV + jnp.arange(TILES_DEV, dtype=jnp.int32)[None, :]
    lower_ids = jnp.roll(halo_send[:, 1, :], 1, axis=0) + (part_ids[:, None] - 1) * TILES_DEV
    upper_ids = jnp.roll(halo_send[:, 0, :], -1, axis=0) + (part_ids[:, None] + 1) * TILES_DEV
    table = jnp.concatenate([local_ids, lower_ids, upper_ids], axis=1).astype(jnp.int32)
    valid = jnp.concatenate([jnp.ones((PARTITIONS, TILES_DEV), dtype=bool), jnp.broadcast_to((part_ids > 0)[:, None], (PARTITIONS, HALO_TILES)), jnp.broadcast_to((part_ids < PARTITIONS - 1)[:, None], (PARTITIONS, HALO_TILES))], axis=1)
    table = jnp.where(valid, table, 0).astype(jnp.int32)
    return (table, valid)

def sweep_tiles(sources, values_flat, target_ids, source_ids, live, transposed):

    def step(summed, entry):
        tile_matrix, target_id, source_id, alive = entry
        source_tile = lax.dynamic_index_in_dim(sources, source_id, 1, keepdims=False).astype(jnp.float32)
        wide_tile = tile_matrix.astype(jnp.float32)
        if transposed:
            term = jnp.einsum('ij,sid->sjd', wide_tile, source_tile)
        else:
            term = jnp.einsum('ij,sjd->sid', wide_tile, source_tile)
        term = jnp.where(alive, term, jnp.zeros_like(term))
        present = lax.dynamic_index_in_dim(summed, target_id, 1, keepdims=True)
        summed = lax.dynamic_update_index_in_dim(summed, present + term[:, None], target_id, 1)
        return (summed, None)
    start = jnp.zeros((SAMPLES, NTILES, TILE, D), jnp.float32)
    summed, unused = lax.scan(step, start, (values_flat, target_ids, source_ids, live))
    return summed

def reference(features, cotangent, weights, gains, tile_pairs, halo_send, entry_counts, tile_values):
    rows_all = SAMPLES * NODES
    table, valid = column_table(halo_send)
    part_ids = jnp.arange(PARTITIONS, dtype=jnp.int32)
    entry_ids = jnp.arange(ENTRIES_DEV, dtype=jnp.int32)
    local_cols = tile_pairs[:, 1, :].astype(jnp.int32)
    rows_global = (part_ids[:, None] * TILES_DEV + tile_pairs[:, 0, :]).reshape(-1).astype(jnp.int32)
    cols_global = jnp.take_along_axis(table, local_cols, axis=1).reshape(-1).astype(jnp.int32)
    live = ((entry_ids[None, :] < entry_counts[:, None]) & jnp.take_along_axis(valid, local_cols, axis=1)).reshape(-1)
    values_flat = tile_values.reshape(PARTITIONS * ENTRIES_DEV, TILE, TILE)
    current = features
    saved = []
    for layer_id in range(LAYERS):
        widened = current.astype(jnp.float32)
        inv_rms = lax.rsqrt(lax.optimization_barrier(jnp.mean(widened * widened, axis=-1, keepdims=True)) + EPSILON)
        normed = (widened * inv_rms * gains[layer_id]).astype(jnp.bfloat16)
        flat_normed = normed.reshape(rows_all, D)
        direct = jnp.dot(flat_normed, weights[layer_id, 0], preferred_element_type=jnp.float32)
        messages = jnp.dot(flat_normed, weights[layer_id, 1], preferred_element_type=jnp.float32).astype(jnp.bfloat16)
        summed = sweep_tiles(messages.reshape(SAMPLES, NTILES, TILE, D), values_flat, rows_global, cols_global, live, False)
        before = direct.reshape(SAMPLES, NODES, D) + summed.reshape(SAMPLES, NODES, D)
        saved.append((widened, inv_rms, flat_normed, before))
        current = (widened + jax.nn.silu(before)).astype(jnp.bfloat16)
    output = current
    upstream = cotangent.astype(jnp.float32)
    grad_blocks = [None] * LAYERS
    gain_rows = [None] * LAYERS
    for layer_id in reversed(range(LAYERS)):
        widened, inv_rms, flat_normed, before = saved[layer_id]
        slope = (upstream * silu_slope(before)).astype(jnp.bfloat16)
        returned = sweep_tiles(slope.reshape(SAMPLES, NTILES, TILE, D), values_flat, cols_global, rows_global, live, True)
        back_messages = returned.astype(jnp.bfloat16).reshape(rows_all, D)
        flat_slope = slope.reshape(rows_all, D)
        dnormed = jnp.dot(flat_slope, weights[layer_id, 0].T, preferred_element_type=jnp.float32) + jnp.dot(back_messages, weights[layer_id, 1].T, preferred_element_type=jnp.float32)
        grad_self = jnp.dot(flat_normed.T, flat_slope, preferred_element_type=jnp.float32)
        grad_other = jnp.dot(flat_normed.T, back_messages, preferred_element_type=jnp.float32)
        grad_blocks[layer_id] = jnp.stack([grad_self, grad_other])
        dnormed = dnormed.reshape(SAMPLES, NODES, D)
        gain_rows[layer_id] = lax.optimization_barrier(jnp.sum(dnormed * widened * inv_rms, axis=(0, 1)))
        if layer_id > 0:
            scaled = dnormed * gains[layer_id]
            mean_part = lax.optimization_barrier(jnp.mean(scaled * widened, axis=-1, keepdims=True))
            upstream = upstream + inv_rms * scaled - widened * (inv_rms * inv_rms * inv_rms) * mean_part
    weight_grads = jnp.transpose(jnp.stack(grad_blocks), (2, 0, 1, 3))
    gain_grads = jnp.stack(gain_rows)
    return (output, weight_grads, gain_grads)
```

```python
import functools

import jax
import jax.numpy as jnp
from jax import lax
from jax.experimental import pallas as pl
from jax.experimental.pallas import tpu as pltpu
from jax.sharding import PartitionSpec as P

MESH = pl.DeviceIdType.MESH
EPSILON = 1e-05
F32 = jnp.float32
BF16 = jnp.bfloat16


def mm(a, b):
    return lax.dot_general(a, b, (((1,), (0,)), ((), ())), preferred_element_type=F32)


def mm_bt(a, b):
    return lax.dot_general(a, b, (((1,), (1,)), ((), ())), preferred_element_type=F32)


def mm_at(a, b):
    return lax.dot_general(a, b, (((0,), (0,)), ((), ())), preferred_element_type=F32)


def kernel(
    nz, nx, chunk, owners,
    x_ref, cot_ref, w_ref, gains_ref, pairs_ref, hs_ref, cnt_ref, tv_ref,
    out_ref, wg_ref, gg_ref,
    wfull, xs, inv_s, normed_s, before_s, adj, adj_t, msgs,
    xsend, xrecv, rsend, rrecv, slope_s, back_s, own_s,
    ga_send, ga_recv, ga_own, gb_send, gb_recv, gb_own, gc_send, gc_recv, gd,
    hg_own, hg_a, hg_b, hg_c,
    w_ss, w_rs, f_ss, f_rs, x_ss, x_rs, r_ss, r_rs,
    a_ss, a_rs, b_ss, b_rs, c_ss, c_rs, d_ss, d_rs, e_ss, e_rs, h_ss, h_rs,
):
    layers, _, width, _ = wfull.shape
    tile = tv_ref.shape[-1]
    tiles = xs.shape[1]
    rows = tiles * tile
    cols = tiles + 2
    half = width // 2
    depth = width // nx
    z = lax.axis_index("nodes")
    xi = lax.axis_index("fsdp")
    r = lax.axis_index("rep")
    sib = {"rep": 1 - r}

    def remote(src, dst, ss, rs, dev):
        return pltpu.make_async_remote_copy(
            src_ref=src, dst_ref=dst, send_sem=ss, recv_sem=rs, device_id=dev, device_id_type=MESH
        )

    def xpeer(d):
        return lax.rem(xi + d, nx)

    def xfrom(d):
        return lax.rem(xi + nx - d, nx)

    def zpeer(d):
        return lax.rem(z + d, nz)

    def zfrom(d):
        return lax.rem(z + nz - d, nz)

    barrier = pltpu.get_barrier_semaphore()
    pl.semaphore_signal(barrier, inc=1, device_id=sib, device_id_type=MESH)
    for d in range(1, nx):
        pl.semaphore_signal(barrier, inc=1, device_id={"fsdp": xpeer(d)}, device_id_type=MESH)
    for d in range(1, nz):
        pl.semaphore_signal(barrier, inc=1, device_id={"nodes": zpeer(d)}, device_id_type=MESH)

    has_low = z > 0
    has_high = z < nz - 1

    def halo(send, recv, ss, rs, l):
        low = remote(send.at[l, 0], recv.at[l, 1], ss.at[l, 0], rs.at[l, 1], {"nodes": jnp.maximum(z - 1, 0)})
        high = remote(send.at[l, 1], recv.at[l, 0], ss.at[l, 1], rs.at[l, 0], {"nodes": jnp.minimum(z + 1, nz - 1)})
        return low, high

    def halo_start(copies):
        pl.when(has_low)(copies[0].start)
        pl.when(has_high)(copies[1].start)

    def halo_wait(copies):
        def low():
            copies[0].wait_send()
            copies[1].wait_recv()

        def high():
            copies[1].wait_send()
            copies[0].wait_recv()

        pl.when(has_low)(low)
        pl.when(has_high)(high)

    xs[0] = x_ref[0].reshape(tiles, tile, width)
    for k, outermost in ((0, z == 0), (1, z == nz - 1)):

        @pl.when(outermost)
        def clear(k=k):
            for l in range(layers):
                xrecv[l, k] = jnp.zeros((tile, width), BF16)
                rrecv[l, k] = jnp.zeros((tile, width), BF16)

    for k in range(2):
        xsend[0, k] = xs[0, hs_ref[0, k, 0]]

    for l in range(layers):
        for w in range(2):
            wfull[l, w, pl.ds(pl.multiple_of(xi * depth, depth), depth), :] = w_ref[l, w]
    pl.semaphore_wait(barrier, 1 + (nx - 1) + (nz - 1))
    xcopies = [halo(xsend, xrecv, x_ss, x_rs, l) for l in range(layers)]
    rcopies = [halo(rsend, rrecv, r_ss, r_rs, l) for l in range(layers)]
    halo_start(xcopies[0])

    def part(l, w, owner):
        return wfull.at[l, w, pl.ds(pl.multiple_of(owner * depth, depth), depth), :]

    gathers = []
    forwards = []
    for l in range(layers):
        for d in range(1, nx):
            g = remote(w_ref.at[l, r], part(l, r, xi), w_ss.at[l, d], w_rs.at[l, d], {"fsdp": xpeer(d)})
            g.start()
            gathers.append(g)
            forwards.append(remote(part(l, r, xfrom(d)), part(l, r, xfrom(d)), f_ss.at[l, d], f_rs.at[l, d], sib))

    count = cnt_ref[0]

    def build(step, carry):
        i = step // cols
        c = lax.rem(step, cols)
        there = jnp.logical_and(
            jnp.logical_or(c != tiles, has_low), jnp.logical_or(c != tiles + 1, has_high)
        )
        total = jnp.zeros((tile, tile), F32)
        for e in range(tv_ref.shape[1]):
            hit = (pairs_ref[0, 0, e] == i) & (pairs_ref[0, 1, e] == c) & (e < count) & there
            total += jnp.where(hit, 1.0, 0.0).astype(F32) * tv_ref[0, e].astype(F32)
        at_i = pl.ds(pl.multiple_of(i * tile, tile), tile)
        at_c = pl.ds(pl.multiple_of(c * tile, tile), tile)
        adj[at_i, at_c] = total.astype(BF16)
        adj_t[at_c, at_i] = total.T.astype(BF16)
        return carry

    lax.fori_loop(0, tiles * cols, build, 0)

    def norm(v, l):
        inv = lax.rsqrt(jnp.mean(v * v, axis=-1, keepdims=True) + EPSILON)
        return inv, (v * inv * gains_ref[l : l + 1, :]).astype(BF16)

    for l in range(layers):
        wide = xs[l].reshape(rows, width).astype(F32)
        inv, normed = norm(wide, l)
        inv_s[l] = inv
        normed_s[l] = normed
        for d in range(nx - 1):
            gathers[l * (nx - 1) + d].wait_recv()
            forwards[l * (nx - 1) + d].start()
        own_first = mm(normed, wfull[l, 0]) if nx == 1 else None
        for d in range(1, nx):
            remote(
                part(l, 1 - r, xfrom(d)), part(l, 1 - r, xfrom(d)), f_ss.at[l, d], f_rs.at[l, d], sib
            ).wait_recv()
        direct = mm(normed, wfull[l, 0]) if own_first is None else own_first
        msgs[0:rows, :] = mm(normed, wfull[l, 1]).astype(BF16)
        halo_wait(xcopies[l])
        _, rim = norm(xrecv[l].reshape(2 * tile, width).astype(F32), l)
        msgs[rows:, :] = mm(rim, wfull[l, 1]).astype(BF16)
        before = direct + mm(adj[...], msgs[...])
        before_s[l] = before
        new = (wide + before / (1.0 + jnp.exp(-before))).astype(BF16)
        if l + 1 < layers:
            xs[l + 1] = new.reshape(tiles, tile, width)
            for k in range(2):
                xsend[l + 1, k] = xs[l + 1, hs_ref[0, k, 0]]
            halo_start(xcopies[l + 1])
        else:
            out_ref[0] = new

    mine = pl.ds(pl.multiple_of(r * half, half), half)
    other = pl.ds(pl.multiple_of((1 - r) * half, half), half)
    blocks = [(l, w) for l in reversed(range(layers)) for w in range(2)]

    a_copies, b_copies, c_copies, d_copies, e_copies = {}, {}, {}, {}, {}

    def stage_a(b):
        l, w = blocks[b]
        source = (slope_s, back_s)[w]
        left = normed_s[l]
        ga_send[b] = mm_at(left, source[l, :, other]).astype(BF16)
        a_copies[b] = remote(ga_send.at[b], ga_recv.at[b], a_ss.at[b], a_rs.at[b], sib)
        a_copies[b].start()
        ga_own[b] = mm_at(left, source[l, :, mine])

    def stage_b(b):
        a_copies[b].wait_recv()
        b_copies[b] = []
        for d in range(1, nx):
            at = pl.ds(pl.multiple_of(xpeer(d) * depth, depth), depth)
            gb_send[b, d] = (ga_own[b, at, :] + ga_recv[b, at, :].astype(F32)).astype(BF16)
            copy = remote(gb_send.at[b, d], gb_recv.at[b, d], b_ss.at[b, d], b_rs.at[b, d], {"fsdp": xpeer(d)})
            copy.start()
            b_copies[b].append(copy)
        at = pl.ds(pl.multiple_of(xi * depth, depth), depth)
        gb_own[b] = ga_own[b, at, :] + ga_recv[b, at, :].astype(F32)

    def span(owner):
        return pl.ds(pl.multiple_of(owner * chunk, chunk), chunk)

    def stage_c(b):
        total = gb_own[b]
        for d in range(1, nx):
            b_copies[b][d - 1].wait_recv()
            total = total + gb_recv[b, d].astype(F32)
        gb_own[b] = total
        gc_send[b] = total.astype(BF16)
        c_copies[b] = []
        for d in range(1, nz):
            to = zpeer(d)
            safe = jnp.minimum(to, owners - 1)
            copy = remote(gc_send.at[b, span(safe), :], gc_recv.at[b, d], c_ss.at[b, d], c_rs.at[b, d], {"nodes": to})
            pl.when(to < owners)(copy.start)
            c_copies[b].append(copy)

    def stage_d(b):
        @pl.when(z < owners)
        def reduce():
            me = jnp.minimum(z, owners - 1)
            total = gb_own[b, span(me), :]
            for d in range(1, nz):
                c_copies[b][d - 1].wait_recv()
                total = total + gc_recv[b, d].astype(F32)
            gd[b, r, span(me), :] = total.astype(BF16)

        d_copies[b] = []
        me = jnp.minimum(z, owners - 1)
        for d in range(1, nz):
            to = zpeer(d)
            copy = remote(
                gd.at[b, r, span(me), :], gd.at[b, r, span(me), :], d_ss.at[b, d], d_rs.at[b, d], {"nodes": to}
            )
            pl.when(z < owners)(copy.start)
            d_copies[b].append(copy)

    def stage_e(b):
        for d in range(1, nz):
            pl.when(zfrom(d) < owners)(d_copies[b][d - 1].wait_recv)
        e_copies[b] = remote(gd.at[b, r], gd.at[b, r], e_ss.at[b], e_rs.at[b], sib)
        e_copies[b].start()
        write(b, r, mine)

    def write(b, c, at):
        l, w = blocks[b]
        wg_ref[:, l, w, at] = gd[b, c].astype(F32)

    def finish(b):
        e_copies[b].wait_recv()
        write(b, 1 - r, other)

    upstream = None
    for l in reversed(range(layers)):
        first = 2 * (layers - 1 - l)
        up = cot_ref[0].astype(F32) if upstream is None else upstream
        before = before_s[l]
        s = 1.0 / (1.0 + jnp.exp(-before))
        slope = (up * (s * (1.0 + before * (1.0 - s)))).astype(BF16)
        slope_s[l] = slope
        rsend[l] = mm(adj_t[rows:, :], slope).astype(BF16).reshape(2, tile, width)
        halo_start(rcopies[l])
        if first > 0:
            stage_a(first - 1)
        stage_a(first)
        own_s[...] = mm(adj_t[0:rows, :], slope)
        dself = mm_bt(slope, wfull[l, 0])
        if first > 0:
            stage_b(first - 1)
            stage_c(first - 2)
        stage_b(first)
        halo_wait(rcopies[l])
        for t in range(tiles):
            at = pl.ds(t * tile, tile)
            part_sum = own_s[at, :]
            for k in range(2):
                part_sum = part_sum + jnp.where(hs_ref[0, k, 0] == t, 1.0, 0.0).astype(F32) * rrecv[l, k].astype(F32)
            back_s[l, at, :] = part_sum.astype(BF16)
        if l == 0:
            stage_a(first + 1)
        dnormed = dself + mm_bt(back_s[l], wfull[l, 1])
        wide = xs[l].reshape(rows, width).astype(F32)
        inv = inv_s[l]
        hg_own[l : l + 1, :] = jnp.sum(dnormed * wide * inv, axis=0, keepdims=True)
        if l > 0:
            scaled = dnormed * gains_ref[l : l + 1, :]
            mean_part = jnp.mean(scaled * wide, axis=-1, keepdims=True)
            upstream = up + inv * scaled - wide * (inv * inv * inv) * mean_part

    ha = remote(hg_own, hg_a, h_ss.at[0], h_rs.at[0], sib)
    ha.start()
    n = len(blocks)
    stage_b(n - 1)
    for b in range(n - 1):
        if b not in c_copies:
            stage_c(b)
    ha.wait_recv()
    hg_b[xi] = hg_own[...] + hg_a[...]
    hb = []
    for d in range(1, nx):
        copy = remote(hg_b.at[xi], hg_b.at[xi], h_ss.at[d], h_rs.at[d], {"fsdp": xpeer(d)})
        copy.start()
        hb.append(copy)
    stage_d(0)
    stage_c(n - 1)
    for d in range(1, nx):
        remote(hg_b.at[xfrom(d)], hg_b.at[xfrom(d)], h_ss.at[d], h_rs.at[d], {"fsdp": xpeer(d)}).wait_recv()
    hsum = hg_b[0]
    for i in range(1, nx):
        hsum = hsum + hg_b[i]
    hg_c[z] = hsum
    hc = []
    for d in range(1, nz):
        copy = remote(hg_c.at[z], hg_c.at[z], h_ss.at[nx + d], h_rs.at[nx + d], {"nodes": zpeer(d)})
        copy.start()
        hc.append(copy)
    for b in range(1, n):
        stage_d(b)
        stage_e(b - 1)
        if b >= 2:
            finish(b - 2)
    stage_e(n - 1)
    finish(n - 2)
    for d in range(1, nz):
        remote(
            hg_c.at[zfrom(d)], hg_c.at[zfrom(d)], h_ss.at[nx + d], h_rs.at[nx + d], {"nodes": zpeer(d)}
        ).wait_recv()
    hsum = hg_c[0]
    for i in range(1, nz):
        hsum = hsum + hg_c[i]
    gg_ref[...] = hsum
    finish(n - 1)

    for g in gathers + forwards + hb + hc + [ha]:
        g.wait_send()
    for b in range(n):
        a_copies[b].wait_send()
        for copy in b_copies[b]:
            copy.wait_send()
        for d in range(1, nz):
            pl.when(zpeer(d) < owners)(c_copies[b][d - 1].wait_send)
            pl.when(z < owners)(d_copies[b][d - 1].wait_send)
        e_copies[b].wait_send()


def solution(mesh):
    nz, nx = mesh.shape["nodes"], mesh.shape["fsdp"]

    def body(features, cotangent, weights, gains, tile_pairs, halo_send, entry_counts, tile_values):
        layers, _, depth, width = weights.shape
        tile = tile_values.shape[-1]
        _, rows, _ = features.shape
        tiles = rows // tile
        cols = tiles + 2
        half = width // 2
        nb = 2 * layers
        chunk = max(16, depth // nz)
        owners = depth // chunk
        vmem = pl.BlockSpec(memory_space=pltpu.VMEM)
        smem = pl.BlockSpec(memory_space=pltpu.SMEM)
        dma = pltpu.SemaphoreType.DMA
        scratch = [
            pltpu.VMEM((layers, 2, width, width), BF16),
            pltpu.VMEM((layers, tiles, tile, width), BF16),
            pltpu.VMEM((layers, rows, 1), F32),
            pltpu.VMEM((layers, rows, width), BF16),
            pltpu.VMEM((layers, rows, width), F32),
            pltpu.VMEM((rows, cols * tile), BF16),
            pltpu.VMEM((cols * tile, rows), BF16),
            pltpu.VMEM((cols * tile, width), BF16),
            pltpu.VMEM((layers, 2, tile, width), BF16),
            pltpu.VMEM((layers, 2, tile, width), BF16),
            pltpu.VMEM((layers, 2, tile, width), BF16),
            pltpu.VMEM((layers, 2, tile, width), BF16),
            pltpu.VMEM((layers, rows, width), BF16),
            pltpu.VMEM((layers, rows, width), BF16),
            pltpu.VMEM((rows, width), F32),
            pltpu.VMEM((nb, width, half), BF16),
            pltpu.VMEM((nb, width, half), BF16),
            pltpu.VMEM((nb, width, half), F32),
            pltpu.VMEM((nb, nx, depth, half), BF16),
            pltpu.VMEM((nb, nx, depth, half), BF16),
            pltpu.VMEM((nb, depth, half), F32),
            pltpu.VMEM((nb, depth, half), BF16),
            pltpu.VMEM((nb, nz, chunk, half), BF16),
            pltpu.VMEM((nb, 2, depth, half), BF16),
            pltpu.VMEM((layers, width), F32),
            pltpu.VMEM((layers, width), F32),
            pltpu.VMEM((nx, layers, width), F32),
            pltpu.VMEM((nz, layers, width), F32),
            dma((layers, nx)), dma((layers, nx)),
            dma((layers, nx)), dma((layers, nx)),
            dma((layers, 2)), dma((layers, 2)),
            dma((layers, 2)), dma((layers, 2)),
            dma((nb,)), dma((nb,)),
            dma((nb, nx)), dma((nb, nx)),
            dma((nb, nz)), dma((nb, nz)),
            dma((nb, nz)), dma((nb, nz)),
            dma((nb,)), dma((nb,)),
            dma((nx + nz,)), dma((nx + nz,)),
        ]
        return pl.pallas_call(
            functools.partial(kernel, nz, nx, chunk, owners),
            out_shape=(
                jax.ShapeDtypeStruct(features.shape, BF16),
                jax.ShapeDtypeStruct((depth, layers, 2, width), F32),
                jax.ShapeDtypeStruct((layers, width), F32),
            ),
            in_specs=[vmem, vmem, vmem, vmem, smem, smem, smem, vmem],
            out_specs=(vmem, vmem, vmem),
            scratch_shapes=scratch,
            compiler_params=pltpu.CompilerParams(
                collective_id=0, has_side_effects=True, vmem_limit_bytes=56 * 1024 * 1024
            ),
        )(features, cotangent, weights, gains, tile_pairs, halo_send, entry_counts, tile_values)

    placed = (
        P(("cases", "fsdp", "rep"), "nodes", None),
        P(("cases", "fsdp", "rep"), "nodes", None),
        P(None, None, "fsdp", None),
        P(),
        P("nodes", None, None),
        P("nodes", None, None),
        P("nodes"),
        P("nodes", None, None, None),
    )
    return jax.shard_map(
        body,
        mesh=mesh,
        in_specs=placed,
        out_specs=(
            P(("cases", "fsdp", "rep"), "nodes", None),
            P("fsdp", "cases", None, None),
            P("cases", None),
        ),
        check_vma=False,
    )
```

```python
import functools

import jax
import jax.numpy as jnp
from jax import lax
from jax.experimental import pallas as pl
from jax.experimental.pallas import tpu as pltpu
from jax.sharding import PartitionSpec as P

MESH = pl.DeviceIdType.MESH
EPSILON = 1e-05
F32 = jnp.float32
BF16 = jnp.bfloat16


def mm(a, b):
    return lax.dot_general(a, b, (((1,), (0,)), ((), ())), preferred_element_type=F32)


def mm_bt(a, b):
    return lax.dot_general(a, b, (((1,), (1,)), ((), ())), preferred_element_type=F32)


def mm_at(a, b):
    return lax.dot_general(a, b, (((0,), (0,)), ((), ())), preferred_element_type=F32)


def kernel(
    nz, nx,
    x_ref, cot_ref, w_ref, gains_ref, pairs_ref, hs_ref, cnt_ref, tv_ref,
    out_ref, gd, gg_ref,
    wfull, xs, inv_s, normed_s, before_s, adj, adj_t, msgs,
    xsend, xrecv, rsend, rrecv, slope_s, back_s, own_s,
    ga_send, ga_recv, ga_own, gb_send, gb_recv, gb_own, z_send, z_recv, z_swap,
    hg_own, hg_a, hg_b, hg_c,
    w_ss, w_rs, f_ss, f_rs, x_ss, x_rs, r_ss, r_rs,
    a_ss, a_rs, b_ss, b_rs, c_ss, c_rs, d_ss, d_rs, e_ss, e_rs, h_ss, h_rs,
):
    layers, _, width, _ = wfull.shape
    tile = tv_ref.shape[-1]
    tiles = xs.shape[1]
    rows = tiles * tile
    cols = tiles + 2
    half = width // 2
    depth = width // nx
    z = lax.axis_index("nodes")
    xi = lax.axis_index("fsdp")
    r = lax.axis_index("rep")
    sib = {"rep": 1 - r}

    def remote(src, dst, ss, rs, dev):
        return pltpu.make_async_remote_copy(
            src_ref=src, dst_ref=dst, send_sem=ss, recv_sem=rs, device_id=dev, device_id_type=MESH
        )

    def xpeer(d):
        return lax.rem(xi + d, nx)

    def xfrom(d):
        return lax.rem(xi + nx - d, nx)

    def zpeer(d):
        return lax.rem(z + d, nz)

    def zfrom(d):
        return lax.rem(z + nz - d, nz)

    barrier = pltpu.get_barrier_semaphore()
    pl.semaphore_signal(barrier, inc=1, device_id=sib, device_id_type=MESH)
    for d in range(1, nx):
        pl.semaphore_signal(barrier, inc=1, device_id={"fsdp": xpeer(d)}, device_id_type=MESH)
    for d in range(1, nz):
        pl.semaphore_signal(barrier, inc=1, device_id={"nodes": zpeer(d)}, device_id_type=MESH)

    has_low = z > 0
    has_high = z < nz - 1

    def halo(send, recv, ss, rs, l):
        low = remote(send.at[l, 0], recv.at[l, 1], ss.at[l, 0], rs.at[l, 1], {"nodes": jnp.maximum(z - 1, 0)})
        high = remote(send.at[l, 1], recv.at[l, 0], ss.at[l, 1], rs.at[l, 0], {"nodes": jnp.minimum(z + 1, nz - 1)})
        return low, high

    def halo_start(copies):
        pl.when(has_low)(copies[0].start)
        pl.when(has_high)(copies[1].start)

    def halo_wait(copies):
        def low():
            copies[0].wait_send()
            copies[1].wait_recv()

        def high():
            copies[1].wait_send()
            copies[0].wait_recv()

        pl.when(has_low)(low)
        pl.when(has_high)(high)

    xs[0] = x_ref[0].reshape(tiles, tile, width)
    for k, outermost in ((0, z == 0), (1, z == nz - 1)):

        @pl.when(outermost)
        def clear(k=k):
            for l in range(layers):
                xrecv[l, k] = jnp.zeros((tile, width), BF16)
                rrecv[l, k] = jnp.zeros((tile, width), BF16)

    for k in range(2):
        xsend[0, k] = xs[0, hs_ref[k]]

    for l in range(layers):
        for w in range(2):
            wfull[l, w, pl.ds(pl.multiple_of(xi * depth, depth), depth), :] = w_ref[l, w]
    pl.semaphore_wait(barrier, 1 + (nx - 1) + (nz - 1))
    xcopies = [halo(xsend, xrecv, x_ss, x_rs, l) for l in range(layers)]
    rcopies = [halo(rsend, rrecv, r_ss, r_rs, l) for l in range(layers)]
    halo_start(xcopies[0])

    def part(l, w, owner):
        return wfull.at[l, w, pl.ds(pl.multiple_of(owner * depth, depth), depth), :]

    gathers = []
    forwards = []
    for l in range(layers):
        for d in range(1, nx):
            g = remote(w_ref.at[l, r], part(l, r, xi), w_ss.at[l, d], w_rs.at[l, d], {"fsdp": xpeer(d)})
            g.start()
            gathers.append(g)
            forwards.append(remote(part(l, r, xfrom(d)), part(l, r, xfrom(d)), f_ss.at[l, d], f_rs.at[l, d], sib))

    count = cnt_ref[0]

    def build(step, carry):
        i = step // cols
        c = lax.rem(step, cols)
        there = jnp.logical_and(
            jnp.logical_or(c != tiles, has_low), jnp.logical_or(c != tiles + 1, has_high)
        )
        total = jnp.zeros((tile, tile), F32)
        for e in range(tv_ref.shape[1]):
            hit = (pairs_ref[0, 0, e] == i) & (pairs_ref[0, 1, e] == c) & (e < count) & there
            total += jnp.where(hit, 1.0, 0.0).astype(F32) * tv_ref[0, e].astype(F32)
        at_i = pl.ds(pl.multiple_of(i * tile, tile), tile)
        at_c = pl.ds(pl.multiple_of(c * tile, tile), tile)
        adj[at_i, at_c] = total.astype(BF16)
        adj_t[at_c, at_i] = total.T.astype(BF16)
        return carry

    lax.fori_loop(0, tiles * cols, build, 0)

    def norm(v, l):
        inv = lax.rsqrt(jnp.mean(v * v, axis=-1, keepdims=True) + EPSILON)
        return inv, (v * inv * gains_ref[l : l + 1, :]).astype(BF16)

    for l in range(layers):
        wide = xs[l].reshape(rows, width).astype(F32)
        inv, normed = norm(wide, l)
        inv_s[l] = inv
        normed_s[l] = normed
        for d in range(nx - 1):
            gathers[l * (nx - 1) + d].wait_recv()
            forwards[l * (nx - 1) + d].start()
        own_first = mm(normed, wfull[l, 0]) if nx == 1 else None
        for d in range(1, nx):
            remote(
                part(l, 1 - r, xfrom(d)), part(l, 1 - r, xfrom(d)), f_ss.at[l, d], f_rs.at[l, d], sib
            ).wait_recv()
        direct = mm(normed, wfull[l, 0]) if own_first is None else own_first
        msgs[0:rows, :] = mm(normed, wfull[l, 1]).astype(BF16)
        halo_wait(xcopies[l])
        _, rim = norm(xrecv[l].reshape(2 * tile, width).astype(F32), l)
        msgs[rows:, :] = mm(rim, wfull[l, 1]).astype(BF16)
        before = direct + mm(adj[...], msgs[...])
        before_s[l] = before
        new = (wide + before / (1.0 + jnp.exp(-before))).astype(BF16)
        if l + 1 < layers:
            xs[l + 1] = new.reshape(tiles, tile, width)
            for k in range(2):
                xsend[l + 1, k] = xs[l + 1, hs_ref[k]]
            halo_start(xcopies[l + 1])
        else:
            out_ref[0] = new

    mine = pl.ds(pl.multiple_of(r * half, half), half)
    other = pl.ds(pl.multiple_of((1 - r) * half, half), half)
    blocks = [(l, w) for l in reversed(range(layers)) for w in range(2)]

    a_copies, b_copies, c_copies, e_copies = {}, {}, {}, {}

    def stage_a(b):
        l, w = blocks[b]
        source = (slope_s, back_s)[w]
        left = normed_s[l]
        ga_send[b] = mm_at(left, source[l, :, other]).astype(BF16)
        a_copies[b] = remote(ga_send.at[b], ga_recv.at[b], a_ss.at[b], a_rs.at[b], sib)
        a_copies[b].start()
        ga_own[b] = mm_at(left, source[l, :, mine])

    def stage_b(b):
        a_copies[b].wait_recv()
        b_copies[b] = []
        for d in range(1, nx):
            at = pl.ds(pl.multiple_of(xpeer(d) * depth, depth), depth)
            gb_send[b, d] = (ga_own[b, at, :] + ga_recv[b, at, :].astype(F32)).astype(BF16)
            copy = remote(gb_send.at[b, d], gb_recv.at[b, d], b_ss.at[b, d], b_rs.at[b, d], {"fsdp": xpeer(d)})
            copy.start()
            b_copies[b].append(copy)
        at = pl.ds(pl.multiple_of(xi * depth, depth), depth)
        gb_own[b] = ga_own[b, at, :] + ga_recv[b, at, :].astype(F32)

    lower_half = z < nz // 2
    outermost = (z == 0) | (z == nz - 1)
    middle = (z == nz // 2 - 1) | (z == nz // 2)
    inner = {"nodes": jnp.where(lower_half, z + 1, z - 1)}
    outer = {"nodes": jnp.clip(jnp.where(lower_half, z - 1, z + 1), 0, nz - 1)}

    def inward(b):
        step = remote(z_send.at[b], z_recv.at[b], c_ss.at[b, 0], c_rs.at[b, 0], inner)
        swap = remote(z_send.at[b], z_swap.at[b], c_ss.at[b, 1], c_rs.at[b, 1], inner)
        return step, swap

    def push(b):
        step, swap = inward(b)
        pl.when(middle)(swap.start)
        pl.when(jnp.logical_not(middle))(step.start)

    def stage_c(b):
        total = gb_own[b]
        for d in range(1, nx):
            b_copies[b][d - 1].wait_recv()
            total = total + gb_recv[b, d].astype(F32)
        gb_own[b] = total

        @pl.when(outermost)
        def begin():
            z_send[b] = total.astype(BF16)
            push(b)

        c_copies[b] = True

    def stage_m(b):
        @pl.when(jnp.logical_not(outermost))
        def add():
            inward(b)[0].wait_recv()
            z_send[b] = (gb_own[b] + z_recv[b].astype(F32)).astype(BF16)
            push(b)

    def outward(b):
        return remote(gd.at[b, r], gd.at[b, r], d_ss.at[b], d_rs.at[b], outer)

    def stage_d(b):
        @pl.when(middle)
        def total():
            inward(b)[1].wait_recv()
            gd[b, r] = (z_send[b].astype(F32) + z_swap[b].astype(F32)).astype(BF16)

        pl.when(jnp.logical_not(middle))(outward(b).wait_recv)
        pl.when(jnp.logical_not(outermost))(outward(b).start)
        e_copies[b] = remote(gd.at[b, r], gd.at[b, r], e_ss.at[b], e_rs.at[b], sib)
        e_copies[b].start()

    def finish(b):
        e_copies[b].wait_recv()

    upstream = None
    for l in reversed(range(layers)):
        first = 2 * (layers - 1 - l)
        up = cot_ref[0].astype(F32) if upstream is None else upstream
        before = before_s[l]
        s = 1.0 / (1.0 + jnp.exp(-before))
        slope = (up * (s * (1.0 + before * (1.0 - s)))).astype(BF16)
        slope_s[l] = slope
        rsend[l] = mm(adj_t[rows:, :], slope).astype(BF16).reshape(2, tile, width)
        halo_start(rcopies[l])
        if first > 0:
            stage_a(first - 1)
        stage_a(first)
        own_s[...] = mm(adj_t[0:rows, :], slope)
        dself = mm_bt(slope, wfull[l, 0])
        if first > 0:
            stage_b(first - 1)
            stage_c(first - 2)
        stage_b(first)
        halo_wait(rcopies[l])
        for t in range(tiles):
            at = pl.ds(t * tile, tile)
            part_sum = own_s[at, :]
            for k in range(2):
                part_sum = part_sum + jnp.where(hs_ref[k] == t, 1.0, 0.0).astype(F32) * rrecv[l, k].astype(F32)
            back_s[l, at, :] = part_sum.astype(BF16)
        if l == 0:
            stage_a(first + 1)
        dnormed = dself + mm_bt(back_s[l], wfull[l, 1])
        wide = xs[l].reshape(rows, width).astype(F32)
        inv = inv_s[l]
        hg_own[l : l + 1, :] = jnp.sum(dnormed * wide * inv, axis=0, keepdims=True)
        if l > 0:
            scaled = dnormed * gains_ref[l : l + 1, :]
            mean_part = jnp.mean(scaled * wide, axis=-1, keepdims=True)
            upstream = up + inv * scaled - wide * (inv * inv * inv) * mean_part

    ha = remote(hg_own, hg_a, h_ss.at[0], h_rs.at[0], sib)
    ha.start()
    n = len(blocks)
    stage_b(n - 1)
    for b in range(n - 1):
        if b not in c_copies:
            stage_c(b)
        if b < n - 2:
            stage_m(b)
    ha.wait_recv()
    hg_b[xi] = hg_own[...] + hg_a[...]
    hb = []
    for d in range(1, nx):
        copy = remote(hg_b.at[xi], hg_b.at[xi], h_ss.at[d], h_rs.at[d], {"fsdp": xpeer(d)})
        copy.start()
        hb.append(copy)
    stage_c(n - 1)
    stage_d(0)
    stage_m(n - 2)
    for d in range(1, nx):
        remote(hg_b.at[xfrom(d)], hg_b.at[xfrom(d)], h_ss.at[d], h_rs.at[d], {"fsdp": xpeer(d)}).wait_recv()
    hsum = hg_b[0]
    for i in range(1, nx):
        hsum = hsum + hg_b[i]
    hg_c[z] = hsum
    hc = []
    for d in range(1, nz):
        copy = remote(hg_c.at[z], hg_c.at[z], h_ss.at[nx + d], h_rs.at[nx + d], {"nodes": zpeer(d)})
        copy.start()
        hc.append(copy)
    stage_d(1)
    stage_m(n - 1)
    for b in range(2, n):
        stage_d(b)
    for b in range(n - 1):
        finish(b)
    for d in range(1, nz):
        remote(
            hg_c.at[zfrom(d)], hg_c.at[zfrom(d)], h_ss.at[nx + d], h_rs.at[nx + d], {"nodes": zpeer(d)}
        ).wait_recv()
    hsum = hg_c[0]
    for i in range(1, nz):
        hsum = hsum + hg_c[i]
    gg_ref[...] = hsum
    finish(n - 1)

    for g in gathers + forwards + hb + hc + [ha]:
        g.wait_send()
    for b in range(n):
        a_copies[b].wait_send()
        for copy in b_copies[b]:
            copy.wait_send()
        step, swap = inward(b)
        pl.when(middle)(swap.wait_send)
        pl.when(jnp.logical_not(middle))(step.wait_send)
        pl.when(jnp.logical_not(outermost))(outward(b).wait_send)
        e_copies[b].wait_send()


def expand_kernel(out_in, gd, gg_in, out_ref, wg_ref, gg_ref):
    out_ref[...] = out_in[...]
    gg_ref[...] = gg_in[...]
    layers, half = wg_ref.shape[1], gd.shape[-1]
    for b in range(gd.shape[0]):
        l, w = layers - 1 - b // 2, b % 2
        for c in range(2):
            wg_ref[:, l, w, c * half : (c + 1) * half] = gd[b, c].astype(F32)


def expand(out, gd, gg):
    nb, _, depth, half = gd.shape
    layers, width = gg.shape
    steps = 4
    rows = pl.BlockSpec((1, out.shape[1] // steps, width), lambda i: (0, i, 0))
    whole = pl.BlockSpec((layers, width), lambda i: (0, 0))
    return pl.pallas_call(
        expand_kernel,
        grid=(steps,),
        out_shape=(
            jax.ShapeDtypeStruct(out.shape, out.dtype),
            jax.ShapeDtypeStruct((depth, layers, 2, width), F32),
            jax.ShapeDtypeStruct(gg.shape, F32),
        ),
        in_specs=[rows, pl.BlockSpec((nb, 2, depth // steps, half), lambda i: (0, 0, i, 0)), whole],
        out_specs=(rows, pl.BlockSpec((depth // steps, layers, 2, width), lambda i: (i, 0, 0, 0)), whole),
    )(out, gd, gg)


def solution(mesh):
    nz, nx = mesh.shape["nodes"], mesh.shape["fsdp"]

    def body(features, cotangent, weights, gains, tile_pairs, halo_send, entry_counts, tile_values):
        layers, _, depth, width = weights.shape
        tile = tile_values.shape[-1]
        _, rows, _ = features.shape
        tiles = rows // tile
        cols = tiles + 2
        half = width // 2
        nb = 2 * layers
        vmem = pl.BlockSpec(memory_space=pltpu.VMEM)
        smem = pl.BlockSpec(memory_space=pltpu.SMEM)
        dma = pltpu.SemaphoreType.DMA
        scratch = [
            pltpu.VMEM((layers, 2, width, width), BF16),
            pltpu.VMEM((layers, tiles, tile, width), BF16),
            pltpu.VMEM((layers, rows, 1), F32),
            pltpu.VMEM((layers, rows, width), BF16),
            pltpu.VMEM((layers, rows, width), F32),
            pltpu.VMEM((rows, cols * tile), BF16),
            pltpu.VMEM((cols * tile, rows), BF16),
            pltpu.VMEM((cols * tile, width), BF16),
            pltpu.VMEM((layers, 2, tile, width), BF16),
            pltpu.VMEM((layers, 2, tile, width), BF16),
            pltpu.VMEM((layers, 2, tile, width), BF16),
            pltpu.VMEM((layers, 2, tile, width), BF16),
            pltpu.VMEM((layers, rows, width), BF16),
            pltpu.VMEM((layers, rows, width), BF16),
            pltpu.VMEM((rows, width), F32),
            pltpu.VMEM((nb, width, half), BF16),
            pltpu.VMEM((nb, width, half), BF16),
            pltpu.VMEM((nb, width, half), F32),
            pltpu.VMEM((nb, nx, depth, half), BF16),
            pltpu.VMEM((nb, nx, depth, half), BF16),
            pltpu.VMEM((nb, depth, half), F32),
            pltpu.VMEM((nb, depth, half), BF16),
            pltpu.VMEM((nb, depth, half), BF16),
            pltpu.VMEM((nb, depth, half), BF16),
            pltpu.VMEM((layers, width), F32),
            pltpu.VMEM((layers, width), F32),
            pltpu.VMEM((nx, layers, width), F32),
            pltpu.VMEM((nz, layers, width), F32),
            dma((layers, nx)), dma((layers, nx)),
            dma((layers, nx)), dma((layers, nx)),
            dma((layers, 2)), dma((layers, 2)),
            dma((layers, 2)), dma((layers, 2)),
            dma((nb,)), dma((nb,)),
            dma((nb, nx)), dma((nb, nx)),
            dma((nb, 2)), dma((nb, 2)),
            dma((nb,)), dma((nb,)),
            dma((nb,)), dma((nb,)),
            dma((nx + nz,)), dma((nx + nz,)),
        ]
        kept = pl.pallas_call(
            functools.partial(kernel, nz, nx),
            out_shape=(
                jax.ShapeDtypeStruct(features.shape, BF16),
                jax.ShapeDtypeStruct((nb, 2, depth, half), BF16),
                jax.ShapeDtypeStruct((layers, width), F32),
            ),
            in_specs=[vmem, vmem, vmem, vmem, smem, smem, smem, vmem],
            out_specs=(vmem, vmem, vmem),
            scratch_shapes=scratch,
            compiler_params=pltpu.CompilerParams(
                collective_id=0, has_side_effects=True, vmem_limit_bytes=56 * 1024 * 1024
            ),
        )(features, cotangent, weights, gains, tile_pairs, halo_send.reshape(-1), entry_counts, tile_values)
        return expand(*kept)

    placed = (
        P(("cases", "fsdp", "rep"), "nodes", None),
        P(("cases", "fsdp", "rep"), "nodes", None),
        P(None, None, "fsdp", None),
        P(),
        P("nodes", None, None),
        P("nodes", None, None),
        P("nodes"),
        P("nodes", None, None, None),
    )
    return jax.shard_map(
        body,
        mesh=mesh,
        in_specs=placed,
        out_specs=(
            P(("cases", "fsdp", "rep"), "nodes", None),
            P("fsdp", "cases", None, None),
            P("cases", None),
        ),
        check_vma=False,
    )
```

```python
import functools

import jax
import jax.numpy as jnp
from jax import lax
from jax.experimental import pallas as pl
from jax.experimental.pallas import tpu as pltpu
from jax.sharding import PartitionSpec as P

MESH = pl.DeviceIdType.MESH
EPSILON = 1e-05
F32 = jnp.float32
BF16 = jnp.bfloat16


def mm(a, b):
    return lax.dot_general(a, b, (((1,), (0,)), ((), ())), preferred_element_type=F32)


def mm_bt(a, b):
    return lax.dot_general(a, b, (((1,), (1,)), ((), ())), preferred_element_type=F32)


def mm_at(a, b):
    return lax.dot_general(a, b, (((0,), (0,)), ((), ())), preferred_element_type=F32)


def kernel(
    nz, nx,
    x_ref, cot_ref, w_ref, gains_ref, pairs_ref, hs_ref, cnt_ref, tv_ref,
    out_ref, gd, gg_ref,
    wfull, xs, inv_s, normed_s, before_s, adj, adj_t, msgs,
    xsend, xrecv, rsend, rrecv, slope_s, back_s, own_s,
    ga_send, ga_recv, ga_own, gb_send, gb_recv, gb_own, z_send, z_recv, z_swap,
    hg_own, hg_a, hg_b, hg_c,
    w_ss, w_rs, f_ss, f_rs, x_ss, x_rs, r_ss, r_rs,
    a_ss, a_rs, b_ss, b_rs, c_ss, c_rs, d_ss, d_rs, e_ss, e_rs, h_ss, h_rs,
):
    layers, _, width, _ = wfull.shape
    tile = tv_ref.shape[-1]
    tiles = xs.shape[1]
    rows = tiles * tile
    cols = tiles + 2
    half = width // 2
    depth = width // nx
    z = lax.axis_index("nodes")
    xi = lax.axis_index("fsdp")
    r = lax.axis_index("rep")
    sib = {"rep": 1 - r}

    def remote(src, dst, ss, rs, dev):
        return pltpu.make_async_remote_copy(
            src_ref=src, dst_ref=dst, send_sem=ss, recv_sem=rs, device_id=dev, device_id_type=MESH
        )

    def xpeer(d):
        return lax.rem(xi + d, nx)

    def xfrom(d):
        return lax.rem(xi + nx - d, nx)

    def zpeer(d):
        return lax.rem(z + d, nz)

    def zfrom(d):
        return lax.rem(z + nz - d, nz)

    barrier = pltpu.get_barrier_semaphore()
    pl.semaphore_signal(barrier, inc=1, device_id=sib, device_id_type=MESH)
    for d in range(1, nx):
        pl.semaphore_signal(barrier, inc=1, device_id={"fsdp": xpeer(d)}, device_id_type=MESH)
    for d in range(1, nz):
        pl.semaphore_signal(barrier, inc=1, device_id={"nodes": zpeer(d)}, device_id_type=MESH)

    has_low = z > 0
    has_high = z < nz - 1

    def halo(send, recv, ss, rs, l):
        low = remote(send.at[l, 0], recv.at[l, 1], ss.at[l, 0], rs.at[l, 1], {"nodes": jnp.maximum(z - 1, 0)})
        high = remote(send.at[l, 1], recv.at[l, 0], ss.at[l, 1], rs.at[l, 0], {"nodes": jnp.minimum(z + 1, nz - 1)})
        return low, high

    def halo_start(copies):
        pl.when(has_low)(copies[0].start)
        pl.when(has_high)(copies[1].start)

    def halo_wait(copies):
        def low():
            copies[0].wait_send()
            copies[1].wait_recv()

        def high():
            copies[1].wait_send()
            copies[0].wait_recv()

        pl.when(has_low)(low)
        pl.when(has_high)(high)

    xs[0] = x_ref[0].reshape(tiles, tile, width)
    for k, outermost in ((0, z == 0), (1, z == nz - 1)):

        @pl.when(outermost)
        def clear(k=k):
            for l in range(layers):
                xrecv[l, k] = jnp.zeros((tile, width), BF16)
                rrecv[l, k] = jnp.zeros((tile, width), BF16)

    for k in range(2):
        xsend[0, k] = xs[0, hs_ref[k]]

    for l in range(layers):
        for w in range(2):
            wfull[l, w, pl.ds(pl.multiple_of(xi * depth, depth), depth), :] = w_ref[l, w]
    pl.semaphore_wait(barrier, 1 + (nx - 1) + (nz - 1))
    xcopies = [halo(xsend, xrecv, x_ss, x_rs, l) for l in range(layers)]
    rcopies = [halo(rsend, rrecv, r_ss, r_rs, l) for l in range(layers)]
    halo_start(xcopies[0])

    def part(l, w, owner):
        return wfull.at[l, w, pl.ds(pl.multiple_of(owner * depth, depth), depth), :]

    gathers = []
    forwards = []
    for l in range(layers):
        for d in range(1, nx):
            g = remote(w_ref.at[l, r], part(l, r, xi), w_ss.at[l, d], w_rs.at[l, d], {"fsdp": xpeer(d)})
            g.start()
            gathers.append(g)
            forwards.append(remote(part(l, r, xfrom(d)), part(l, r, xfrom(d)), f_ss.at[l, d], f_rs.at[l, d], sib))

    count = cnt_ref[0]

    def build(step, carry):
        i = step // cols
        c = lax.rem(step, cols)
        there = jnp.logical_and(
            jnp.logical_or(c != tiles, has_low), jnp.logical_or(c != tiles + 1, has_high)
        )
        total = jnp.zeros((tile, tile), F32)
        for e in range(tv_ref.shape[1]):
            hit = (pairs_ref[0, 0, e] == i) & (pairs_ref[0, 1, e] == c) & (e < count) & there
            total += jnp.where(hit, 1.0, 0.0).astype(F32) * tv_ref[0, e].astype(F32)
        at_i = pl.ds(pl.multiple_of(i * tile, tile), tile)
        at_c = pl.ds(pl.multiple_of(c * tile, tile), tile)
        adj[at_i, at_c] = total.astype(BF16)
        adj_t[at_c, at_i] = total.T.astype(BF16)
        return carry

    lax.fori_loop(0, tiles * cols, build, 0)

    def norm(v, l):
        inv = lax.rsqrt(jnp.mean(v * v, axis=-1, keepdims=True) + EPSILON)
        return inv, (v * inv * gains_ref[l : l + 1, :]).astype(BF16)

    for l in range(layers):
        wide = xs[l].reshape(rows, width).astype(F32)
        inv, normed = norm(wide, l)
        inv_s[l] = inv
        normed_s[l] = normed
        for d in range(nx - 1):
            gathers[l * (nx - 1) + d].wait_recv()
            forwards[l * (nx - 1) + d].start()
        own_first = mm(normed, wfull[l, 0]) if nx == 1 else None
        for d in range(1, nx):
            remote(
                part(l, 1 - r, xfrom(d)), part(l, 1 - r, xfrom(d)), f_ss.at[l, d], f_rs.at[l, d], sib
            ).wait_recv()
        direct = mm(normed, wfull[l, 0]) if own_first is None else own_first
        msgs[0:rows, :] = mm(normed, wfull[l, 1]).astype(BF16)
        halo_wait(xcopies[l])
        _, rim = norm(xrecv[l].reshape(2 * tile, width).astype(F32), l)
        msgs[rows:, :] = mm(rim, wfull[l, 1]).astype(BF16)
        before = direct + mm(adj[...], msgs[...])
        before_s[l] = before
        new = (wide + before / (1.0 + jnp.exp(-before))).astype(BF16)
        if l + 1 < layers:
            xs[l + 1] = new.reshape(tiles, tile, width)
            for k in range(2):
                xsend[l + 1, k] = xs[l + 1, hs_ref[k]]
            halo_start(xcopies[l + 1])
        else:
            out_ref[0] = new

    mine = pl.ds(pl.multiple_of(r * half, half), half)
    other = pl.ds(pl.multiple_of((1 - r) * half, half), half)
    blocks = [(l, w) for l in reversed(range(layers)) for w in range(2)]

    a_copies, b_copies, c_copies, e_copies = {}, {}, {}, {}
    m_done = set()

    def stage_a(b):
        l, w = blocks[b]
        source = (slope_s, back_s)[w]
        left = normed_s[l]
        ga_send[b] = mm_at(left, source[l, :, other]).astype(BF16)
        a_copies[b] = remote(ga_send.at[b], ga_recv.at[b], a_ss.at[b], a_rs.at[b], sib)
        a_copies[b].start()
        ga_own[b] = mm_at(left, source[l, :, mine])

    def stage_b(b):
        a_copies[b].wait_recv()
        b_copies[b] = []
        for d in range(1, nx):
            at = pl.ds(pl.multiple_of(xpeer(d) * depth, depth), depth)
            gb_send[b, d] = (ga_own[b, at, :] + ga_recv[b, at, :].astype(F32)).astype(BF16)
            copy = remote(gb_send.at[b, d], gb_recv.at[b, d], b_ss.at[b, d], b_rs.at[b, d], {"fsdp": xpeer(d)})
            copy.start()
            b_copies[b].append(copy)
        at = pl.ds(pl.multiple_of(xi * depth, depth), depth)
        gb_own[b] = ga_own[b, at, :] + ga_recv[b, at, :].astype(F32)

    lower_half = z < nz // 2
    outermost = (z == 0) | (z == nz - 1)
    middle = (z == nz // 2 - 1) | (z == nz // 2)
    inner = {"nodes": jnp.where(lower_half, z + 1, z - 1)}
    outer = {"nodes": jnp.clip(jnp.where(lower_half, z - 1, z + 1), 0, nz - 1)}

    pieces = [slice(h * depth // 2, (h + 1) * depth // 2) for h in range(2)]

    def inward(b, h):
        at = pieces[h]
        step = remote(z_send.at[b, at], z_recv.at[b, at], c_ss.at[b, h], c_rs.at[b, h], inner)
        swap = remote(z_send.at[b, at], z_swap.at[b, at], c_ss.at[b, 2 + h], c_rs.at[b, 2 + h], inner)
        return step, swap

    def push(b, h):
        step, swap = inward(b, h)
        pl.when(middle)(swap.start)
        pl.when(jnp.logical_not(middle))(step.start)

    def stage_c(b):
        total = gb_own[b]
        for d in range(1, nx):
            b_copies[b][d - 1].wait_recv()
            total = total + gb_recv[b, d].astype(F32)
        gb_own[b] = total

        @pl.when(outermost)
        def begin():
            z_send[b] = total.astype(BF16)
            for h in range(2):
                push(b, h)

        c_copies[b] = True

    def stage_m(b):
        m_done.add(b)

        @pl.when(jnp.logical_not(outermost))
        def add():
            for h, at in enumerate(pieces):
                inward(b, h)[0].wait_recv()
                z_send[b, at] = (gb_own[b, at] + z_recv[b, at].astype(F32)).astype(BF16)
                push(b, h)

    def outward(b, h):
        place = gd.at[b, r, pieces[h]]
        return remote(place, place, d_ss.at[b, h], d_rs.at[b, h], outer)

    def stage_d(b):
        e_copies[b] = []
        for h, at in enumerate(pieces):

            @pl.when(middle)
            def total(h=h, at=at):
                inward(b, h)[1].wait_recv()
                gd[b, r, at] = (z_send[b, at].astype(F32) + z_swap[b, at].astype(F32)).astype(BF16)

            pl.when(jnp.logical_not(middle))(outward(b, h).wait_recv)
            pl.when(jnp.logical_not(outermost))(outward(b, h).start)
            place = gd.at[b, r, at]
            copy = remote(place, place, e_ss.at[b, h], e_rs.at[b, h], sib)
            copy.start()
            e_copies[b].append(copy)

    def finish(b):
        for copy in e_copies[b]:
            copy.wait_recv()

    upstream = None
    for l in reversed(range(layers)):
        first = 2 * (layers - 1 - l)
        up = cot_ref[0].astype(F32) if upstream is None else upstream
        before = before_s[l]
        s = 1.0 / (1.0 + jnp.exp(-before))
        slope = (up * (s * (1.0 + before * (1.0 - s)))).astype(BF16)
        slope_s[l] = slope
        rsend[l] = mm(adj_t[rows:, :], slope).astype(BF16).reshape(2, tile, width)
        halo_start(rcopies[l])
        if first > 0:
            stage_a(first - 1)
        stage_a(first)
        own_s[...] = mm(adj_t[0:rows, :], slope)
        dself = mm_bt(slope, wfull[l, 0])
        if first > 0:
            stage_b(first - 1)
            stage_c(first - 2)
        stage_b(first)
        halo_wait(rcopies[l])
        for t in range(tiles):
            at = pl.ds(t * tile, tile)
            part_sum = own_s[at, :]
            for k in range(2):
                part_sum = part_sum + jnp.where(hs_ref[k] == t, 1.0, 0.0).astype(F32) * rrecv[l, k].astype(F32)
            back_s[l, at, :] = part_sum.astype(BF16)
        if l == 0:
            stage_a(first + 1)
        if first > 0:
            stage_c(first - 1)
            stage_m(first - 2)
        dnormed = dself + mm_bt(back_s[l], wfull[l, 1])
        wide = xs[l].reshape(rows, width).astype(F32)
        inv = inv_s[l]
        hg_own[l : l + 1, :] = jnp.sum(dnormed * wide * inv, axis=0, keepdims=True)
        if l > 0:
            scaled = dnormed * gains_ref[l : l + 1, :]
            mean_part = jnp.mean(scaled * wide, axis=-1, keepdims=True)
            upstream = up + inv * scaled - wide * (inv * inv * inv) * mean_part

    ha = remote(hg_own, hg_a, h_ss.at[0], h_rs.at[0], sib)
    ha.start()
    n = len(blocks)
    stage_b(n - 1)
    for b in range(n - 1):
        if b not in c_copies:
            stage_c(b)
        if b < n - 2 and b not in m_done:
            stage_m(b)
    ha.wait_recv()
    hg_b[xi] = hg_own[...] + hg_a[...]
    hb = []
    for d in range(1, nx):
        copy = remote(hg_b.at[xi], hg_b.at[xi], h_ss.at[d], h_rs.at[d], {"fsdp": xpeer(d)})
        copy.start()
        hb.append(copy)
    stage_c(n - 1)
    stage_d(0)
    stage_m(n - 2)
    for d in range(1, nx):
        remote(hg_b.at[xfrom(d)], hg_b.at[xfrom(d)], h_ss.at[d], h_rs.at[d], {"fsdp": xpeer(d)}).wait_recv()
    hsum = hg_b[0]
    for i in range(1, nx):
        hsum = hsum + hg_b[i]
    hg_c[z] = hsum
    hc = []
    for d in range(1, nz):
        copy = remote(hg_c.at[z], hg_c.at[z], h_ss.at[nx + d], h_rs.at[nx + d], {"nodes": zpeer(d)})
        copy.start()
        hc.append(copy)
    stage_d(1)
    stage_m(n - 1)
    for b in range(2, n):
        stage_d(b)
    for b in range(n - 1):
        finish(b)
    for d in range(1, nz):
        remote(
            hg_c.at[zfrom(d)], hg_c.at[zfrom(d)], h_ss.at[nx + d], h_rs.at[nx + d], {"nodes": zpeer(d)}
        ).wait_recv()
    hsum = hg_c[0]
    for i in range(1, nz):
        hsum = hsum + hg_c[i]
    gg_ref[...] = hsum
    finish(n - 1)

    for g in gathers + forwards + hb + hc + [ha]:
        g.wait_send()
    for b in range(n):
        a_copies[b].wait_send()
        for copy in b_copies[b]:
            copy.wait_send()
        for h in range(2):
            step, swap = inward(b, h)
            pl.when(middle)(swap.wait_send)
            pl.when(jnp.logical_not(middle))(step.wait_send)
            pl.when(jnp.logical_not(outermost))(outward(b, h).wait_send)
            e_copies[b][h].wait_send()


def expand_kernel(out_in, gd, gg_in, out_ref, wg_ref, gg_ref):
    out_ref[...] = out_in[...]
    gg_ref[...] = gg_in[...]
    layers, half = wg_ref.shape[1], gd.shape[-1]
    for b in range(gd.shape[0]):
        l, w = layers - 1 - b // 2, b % 2
        for c in range(2):
            wg_ref[:, l, w, c * half : (c + 1) * half] = gd[b, c].astype(F32)


def expand(out, gd, gg):
    nb, _, depth, half = gd.shape
    layers, width = gg.shape
    steps = 4
    rows = pl.BlockSpec((1, out.shape[1] // steps, width), lambda i: (0, i, 0))
    whole = pl.BlockSpec((layers, width), lambda i: (0, 0))
    return pl.pallas_call(
        expand_kernel,
        grid=(steps,),
        out_shape=(
            jax.ShapeDtypeStruct(out.shape, out.dtype),
            jax.ShapeDtypeStruct((depth, layers, 2, width), F32),
            jax.ShapeDtypeStruct(gg.shape, F32),
        ),
        in_specs=[rows, pl.BlockSpec((nb, 2, depth // steps, half), lambda i: (0, 0, i, 0)), whole],
        out_specs=(rows, pl.BlockSpec((depth // steps, layers, 2, width), lambda i: (i, 0, 0, 0)), whole),
    )(out, gd, gg)


def solution(mesh):
    nz, nx = mesh.shape["nodes"], mesh.shape["fsdp"]

    def body(features, cotangent, weights, gains, tile_pairs, halo_send, entry_counts, tile_values):
        layers, _, depth, width = weights.shape
        tile = tile_values.shape[-1]
        _, rows, _ = features.shape
        tiles = rows // tile
        cols = tiles + 2
        half = width // 2
        nb = 2 * layers
        vmem = pl.BlockSpec(memory_space=pltpu.VMEM)
        smem = pl.BlockSpec(memory_space=pltpu.SMEM)
        dma = pltpu.SemaphoreType.DMA
        scratch = [
            pltpu.VMEM((layers, 2, width, width), BF16),
            pltpu.VMEM((layers, tiles, tile, width), BF16),
            pltpu.VMEM((layers, rows, 1), F32),
            pltpu.VMEM((layers, rows, width), BF16),
            pltpu.VMEM((layers, rows, width), F32),
            pltpu.VMEM((rows, cols * tile), BF16),
            pltpu.VMEM((cols * tile, rows), BF16),
            pltpu.VMEM((cols * tile, width), BF16),
            pltpu.VMEM((layers, 2, tile, width), BF16),
            pltpu.VMEM((layers, 2, tile, width), BF16),
            pltpu.VMEM((layers, 2, tile, width), BF16),
            pltpu.VMEM((layers, 2, tile, width), BF16),
            pltpu.VMEM((layers, rows, width), BF16),
            pltpu.VMEM((layers, rows, width), BF16),
            pltpu.VMEM((rows, width), F32),
            pltpu.VMEM((nb, width, half), BF16),
            pltpu.VMEM((nb, width, half), BF16),
            pltpu.VMEM((nb, width, half), F32),
            pltpu.VMEM((nb, nx, depth, half), BF16),
            pltpu.VMEM((nb, nx, depth, half), BF16),
            pltpu.VMEM((nb, depth, half), F32),
            pltpu.VMEM((nb, depth, half), BF16),
            pltpu.VMEM((nb, depth, half), BF16),
            pltpu.VMEM((nb, depth, half), BF16),
            pltpu.VMEM((layers, width), F32),
            pltpu.VMEM((layers, width), F32),
            pltpu.VMEM((nx, layers, width), F32),
            pltpu.VMEM((nz, layers, width), F32),
            dma((layers, nx)), dma((layers, nx)),
            dma((layers, nx)), dma((layers, nx)),
            dma((layers, 2)), dma((layers, 2)),
            dma((layers, 2)), dma((layers, 2)),
            dma((nb,)), dma((nb,)),
            dma((nb, nx)), dma((nb, nx)),
            dma((nb, 4)), dma((nb, 4)),
            dma((nb, 2)), dma((nb, 2)),
            dma((nb, 2)), dma((nb, 2)),
            dma((nx + nz,)), dma((nx + nz,)),
        ]
        kept = pl.pallas_call(
            functools.partial(kernel, nz, nx),
            out_shape=(
                jax.ShapeDtypeStruct(features.shape, BF16),
                jax.ShapeDtypeStruct((nb, 2, depth, half), BF16),
                jax.ShapeDtypeStruct((layers, width), F32),
            ),
            in_specs=[vmem, vmem, vmem, vmem, smem, smem, smem, vmem],
            out_specs=(vmem, vmem, vmem),
            scratch_shapes=scratch,
            compiler_params=pltpu.CompilerParams(
                collective_id=0, has_side_effects=True, vmem_limit_bytes=56 * 1024 * 1024
            ),
        )(features, cotangent, weights, gains, tile_pairs, halo_send.reshape(-1), entry_counts, tile_values)
        return expand(*kept)

    placed = (
        P(("cases", "fsdp", "rep"), "nodes", None),
        P(("cases", "fsdp", "rep"), "nodes", None),
        P(None, None, "fsdp", None),
        P(),
        P("nodes", None, None),
        P("nodes", None, None),
        P("nodes"),
        P("nodes", None, None, None),
    )
    return jax.shard_map(
        body,
        mesh=mesh,
        in_specs=placed,
        out_specs=(
            P(("cases", "fsdp", "rep"), "nodes", None),
            P("fsdp", "cases", None, None),
            P("cases", None),
        ),
        check_vma=False,
    )
```
